512 devices in a mesh: gx: 8 (over y), gy: 8 (over z_lo, core), gz: 8 (over x, z_hi).
Axes of the slice: x: 4, y: 8, z: 8 (z_hi: 2, z_lo: 4; z = z_hi * 4 + z_lo), core: 2. Of those that a mesh axis runs over, the one named last changes fastest.
Arguments:
- inputs: bfloat16 [2048, 4096], P('gx', 'gy'), may hold values from -6 to 6
- out_grad: bfloat16 [2048, 4096], P('gx', 'gy'), may hold values from -6 to 6
- gate_act: bfloat16 [2048, 14336], P('gx', 'gz'), may hold values from -7 to 7
- up_act: bfloat16 [2048, 14336], P('gx', 'gz'), may hold values from -6 to 6
- gate_weight: bfloat16 [4096, 14336], P('gy', ('gz', 'gx')), may hold values from -0.09375 to 0.09375
- up_weight: bfloat16 [4096, 14336], P('gy', ('gz', 'gx')), may hold values from -0.09375 to 0.09375
- down_weight: bfloat16 [14336, 4096], P(('gz', 'gx'), 'gy'), may hold values from -0.046875 to 0.046875
Outputs:
- input_grad: bfloat16 [2048, 4096], P('gx', ('gy', 'gz'))
- gate_weight_grad: float32 [4096, 14336], P('gy', ('gz', 'gx'))
- up_weight_grad: float32 [4096, 14336], P('gy', ('gz', 'gx'))
- down_weight_grad: float32 [14336, 4096], P(('gz', 'gx'), 'gy')
The draws below stay inside these ranges and needn't reach their ends.
All inputs are finite; a program needn't handle non-finite values.
Results may differ from the reference program's by a relative error of at most 0.025.
Values may be sent and summed in bfloat16 or wider, within the bound.
A program may use at most 64 MiB of HBM per device.

```python
import jax
import jax.numpy as jnp
from jax import lax

D = 4096
FF = 14336
TOKENS = 2048
N_GY = 8


def block_levels(stream_key, shape, cuts, smallest, high):
    level, own = 1.0, jax.random.fold_in(stream_key, 6)
    for dim, parts in cuts:
        heights = jnp.exp(jax.random.uniform(jax.random.fold_in(own, dim), (parts,), jnp.float32, smallest / len(cuts), high / len(cuts)))
        level = level * jnp.repeat(heights, shape[dim] // parts).reshape([-1 if axis == dim else 1 for axis in range(len(shape))])
    return level


def bell_draw(key, dims, deviation, limit, cuts=(), kind=jnp.bfloat16):
    array = deviation * jax.random.normal(key, dims, jnp.float32)
    if cuts:
        array = array * block_levels(key, dims, cuts, -0.22, 0.18)
    return jnp.clip(array, -limit, limit).astype(kind)


def setup_inputs(seed: int = 0) -> dict:
    keys = jax.random.split(jax.random.key(seed), 8)
    inputs = bell_draw(keys[0], (TOKENS, D), 1.0, 6.0, ((0, 8), (1, 8)))
    out_grad = bell_draw(keys[1], (TOKENS, D), 1.0, 6.0, ((0, 8), (1, 8)))
    gate_act = bell_draw(keys[2], (TOKENS, FF), 1.5, 7.0, ((0, 8), (1, 8)))
    up_act = bell_draw(keys[3], (TOKENS, FF), 1.0, 6.0, ((0, 8), (1, 8)))
    gate_weight = bell_draw(keys[4], (D, FF), D ** -0.5, 0.09375, ((0, 8), (1, 64)))
    up_weight = bell_draw(keys[5], (D, FF), D ** -0.5, 0.09375, ((0, 8), (1, 64)))
    down_weight = bell_draw(keys[6], (FF, D), FF ** -0.5, 0.046875, ((0, 64), (1, 8)))
    return {"inputs": inputs, "out_grad": out_grad, "gate_act": gate_act, "up_act": up_act, "gate_weight": gate_weight, "up_weight": up_weight, "down_weight": down_weight}


def reference(inputs, out_grad, gate_act, up_act, gate_weight, up_weight, down_weight):
    gate_full = gate_act.astype(jnp.float32)
    up_full = up_act.astype(jnp.float32)
    sigma = jax.nn.sigmoid(gate_full)
    silu_gate = gate_full * sigma
    hidden = (silu_gate * up_full).astype(jnp.bfloat16)
    block_width = D // N_GY
    hidden_grad = jnp.zeros((out_grad.shape[0], down_weight.shape[0]), jnp.float32)
    for block in range(N_GY):
        lower = block * block_width
        term = jnp.dot(out_grad[:, lower:lower + block_width], down_weight[:, lower:lower + block_width].T, preferred_element_type=jnp.float32)
        rounded = lax.optimization_barrier(term.astype(jnp.bfloat16))
        hidden_grad = hidden_grad + rounded.astype(jnp.float32)
    gate_grad = (hidden_grad * up_full * sigma * (1.0 + gate_full * (1.0 - sigma))).astype(jnp.bfloat16)
    up_grad = (hidden_grad * silu_gate).astype(jnp.bfloat16)
    input_grad = jnp.dot(gate_grad, gate_weight.T, preferred_element_type=jnp.float32)
    input_grad = input_grad + jnp.dot(up_grad, up_weight.T, preferred_element_type=jnp.float32)
    gate_weight_grad = jnp.dot(inputs.T, gate_grad, preferred_element_type=jnp.float32)
    up_weight_grad = jnp.dot(inputs.T, up_grad, preferred_element_type=jnp.float32)
    down_weight_grad = jnp.dot(hidden.T, out_grad, preferred_element_type=jnp.float32)
    return (input_grad.astype(jnp.bfloat16), gate_weight_grad, up_weight_grad, down_weight_grad)
```

```python
import jax
import jax.numpy as jnp
from jax import lax
from jax.experimental import pallas as pl
from jax.experimental.pallas import tpu as pltpu
from jax.sharding import PartitionSpec as P

MESH = pl.DeviceIdType.MESH
BF = jnp.bfloat16
F32 = jnp.float32
N = 8
ROWS = 128
SUB = 32
NT = (((1,), (1,)), ((), ()))
TN = (((0,), (0,)), ((), ()))


def kernel(
    og, inp, gact, uact, gw, uw, dw,
    out_in, out_gate, out_up, out_down,
    og_all, inp_all, gw_v, uw_v, dw_v, araw, ast, act,
    tbuf, trecv, sbuf, zrecv, grads, hid, pbuf, xrecv, fbuf, yrecv, rbuf, hrecv,
    load_sem, og_s, og_r, in_s, in_r, act_s, act_r, t_s, t_r, z_s, z_r,
    g_s, g_r, gc_s, gc_r, x_s, x_r, f_s, f_r, h_s, h_r, hc_s, hc_r, e_s, e_r,
):
    a, b, c = (lax.axis_index(n) for n in ("gx", "gy", "gz"))
    core, zl = lax.rem(b, 2), lax.div(b, 2)
    x, zh = lax.div(c, 2), lax.rem(c, 2)
    cols = dw.shape[0]

    def y_peer(step):
        return (lax.rem(a + step + N, N), b, c)

    partner = (a, b + 1 - 2 * core, c)
    far = (a, b, c + 1 - 2 * zh)

    def z_peer(i):
        return (a, 2 * lax.rem(zl + i, 4) + core, c)

    def x_peer(i):
        return (a, b, 2 * lax.rem(x + i, 4) + zh)

    def remote(src, dst, s, r, to):
        return pltpu.make_async_remote_copy(
            src_ref=src, dst_ref=dst, send_sem=s, recv_sem=r, device_id=to, device_id_type=MESH
        )

    loads = []
    for h in range(2):
        loads.append((og.at[pl.ds(h * ROWS, ROWS)], og_all.at[0, h]))
    loads.append((dw, dw_v))
    for h in range(2):
        rows = pl.ds(pl.multiple_of(h * ROWS + zl * SUB, SUB), SUB)
        loads.append((gact.at[rows], araw.at[0, h]))
        loads.append((uact.at[rows], araw.at[1, h]))
    loads.append((gw, gw_v))
    loads.append((uw, uw_v))
    for h in range(2):
        loads.append((inp.at[pl.ds(h * ROWS, ROWS)], inp_all.at[0, h]))
    loads = [pltpu.make_async_copy(s, d, load_sem.at[i]) for i, (s, d) in enumerate(loads)]
    for copy in loads:
        copy.start()

    barrier = pltpu.get_barrier_semaphore()
    peers = [y_peer(i) for i in range(1, N)] + [z_peer(i) for i in range(1, 4)]
    peers += [x_peer(i) for i in range(1, 4)] + [partner, far]
    for peer in peers:
        pl.semaphore_signal(barrier, inc=1, device_id=peer, device_id_type=MESH)
    pl.semaphore_wait(barrier, len(peers))

    def ring(buf, s, r, m, side):
        src = buf.at[0, (m - 1 + side) % 2] if isinstance(m, int) and m <= 2 else buf.at[m - 2, side]
        return remote(src, buf.at[m, side], s.at[m, side], r.at[m, side], y_peer(1 - 2 * side))

    def og_ring(m, side):
        return ring(og_all, og_s, og_r, m, side)

    def in_ring(m, side):
        return ring(inp_all, in_s, in_r, m, side)

    def act_copy(j):
        to = y_peer((1 - 2 * core) * ((j + 1) // 2))
        return remote(ast.at[to[0], lax.rem(core + j - 1, 2)], act.at[j], act_s.at[j], act_r.at[j], to)

    def t_copy(j):
        return remote(tbuf.at[j, 1 - core], trecv.at[j], t_s.at[j], t_r.at[j], partner)

    def z_copy(j, i):
        to = lax.rem(zl + i, 4)
        return remote(sbuf.at[j, to], zrecv.at[j, zl], z_s.at[j, i], z_r.at[j, i], z_peer(i))

    def g_copy(j, i):
        mine = grads.at[j, :, core, zl]
        return remote(mine, mine, g_s.at[j, i], g_r.at[j, i], z_peer(i))

    def gc_copy(j):
        mine = grads.at[j, :, core]
        return remote(mine, mine, gc_s.at[j], gc_r.at[j], partner)

    def x_copy(j, i):
        to = lax.rem(x + i, 4)
        return remote(pbuf.at[j, to], xrecv.at[j, x], x_s.at[j, i], x_r.at[j, i], x_peer(i))

    def f_copy(j, side):
        step = ((j + 1) // 2) * (2 * side - 1)
        return remote(fbuf.at[j, side], yrecv.at[j, side], f_s.at[j, side], f_r.at[j, side], y_peer(step))

    def h_copy(i):
        mine = hid.at[:, core, zl]
        return remote(mine, mine, h_s.at[i], h_r.at[i], z_peer(i))

    def hc_copy():
        mine = hid.at[:, core]
        return remote(mine, mine, hc_s.at[0], hc_r.at[0], partner)

    def e_copy():
        return remote(rbuf.at[1 - zh], hrecv, e_s.at[0], e_r.at[0], far)

    def stage_terms(j):
        term = lax.dot_general(
            og_all[j].reshape(2 * ROWS, -1), dw_v[...], NT, preferred_element_type=F32
        )
        tbuf[j] = term.astype(BF).reshape(2, ROWS, cols)
        t_copy(j).start()

    def stage_pair(j):
        t_copy(j).wait_recv()
        total = tbuf[j, core].astype(F32) + trecv[j].astype(F32)
        sbuf[j] = total.astype(BF).reshape(4, SUB, cols)
        for i in range(1, 4):
            z_copy(j, i).start()

    def stage_act(j):
        for i in range(1, 4):
            z_copy(j, i).wait_recv()
        own = sbuf[j, zl]
        zrecv[j, zl] = own
        hidden_grad = zrecv[j, 0].astype(F32)
        for i in range(1, 4):
            hidden_grad += zrecv[j, i].astype(F32)
        gate, up = act[j, 0].astype(F32), act[j, 1].astype(F32)
        sigma = jax.nn.sigmoid(gate)
        silu = gate * sigma
        grads[j, 0, core, zl] = (hidden_grad * up * sigma * (1.0 + gate * (1.0 - sigma))).astype(BF)
        grads[j, 1, core, zl] = (hidden_grad * silu).astype(BF)
        hid[j, core, zl] = (silu * up).astype(BF)
        for i in range(1, 4):
            g_copy(j, i).start()

    def stage_share(j):
        for i in range(1, 4):
            g_copy(j, i).wait_recv()
        gc_copy(j).start()

    def stage_input(j):
        gc_copy(j).wait_recv()
        part = lax.dot_general(
            grads[j, 0].reshape(2 * ROWS, cols), gw_v[...], NT, preferred_element_type=F32
        ) + lax.dot_general(
            grads[j, 1].reshape(2 * ROWS, cols), uw_v[...], NT, preferred_element_type=F32
        )
        for i in range(4):
            pbuf[j, i] = part[:, i * 128:(i + 1) * 128].astype(BF).reshape(2, ROWS, 128)
        for i in range(1, 4):
            x_copy(j, i).start()

    def stage_columns(j):
        for i in range(1, 4):
            x_copy(j, i).wait_recv()
        xrecv[j, x] = pbuf[j, x]
        total = xrecv[j, 0].astype(F32)
        for i in range(1, 4):
            total += xrecv[j, i].astype(F32)
        if isinstance(j, int) and j == 0:
            yrecv[0] = total.astype(BF)
        else:
            fbuf[j] = total.astype(BF)
            for side in range(2):
                f_copy(j, side).start()

    def stage_weights(j):
        block = inp_all[j].reshape(2 * ROWS, -1)
        gate = lax.dot_general(block, grads[j, 0].reshape(2 * ROWS, cols), TN, preferred_element_type=F32)
        up = lax.dot_general(block, grads[j, 1].reshape(2 * ROWS, cols), TN, preferred_element_type=F32)
        if isinstance(j, int) and j == 0:
            out_gate[...] = gate
            out_up[...] = up
        else:
            out_gate[...] += gate
            out_up[...] += up

    def stage_owner():
        for j in range(1, N):
            for side in range(2):
                f_copy(j, side).wait_recv()
        for half in range(2):
            total = yrecv[0, half].astype(F32)
            for j in range(1, N):
                total += yrecv[j, (j - 1 + half) % 2].astype(F32)
            for i in range(2):
                rbuf[i, pl.ds(half * ROWS, ROWS)] = total[:, i * 64:(i + 1) * 64].astype(BF)
        e_copy().start()

    for i in range(3):
        loads[i].wait()
    for m in (1, 2):
        for side in range(2):
            og_ring(m, side).start()
    stage_terms(0)
    for i in range(3, 7):
        loads[i].wait()
    for kind in range(2):
        for h in range(2):
            block = araw[kind, h]
            for i in range(N):
                ast[i, h, kind] = block[:, i * cols:(i + 1) * cols]
    act[0] = ast[a, core]
    for j in range(1, N):
        act_copy(j).start()
    stage_pair(0)

    def tick(t):
        if 1 <= t < N:
            for side in range(2):
                og_ring(t, side).wait_recv()
            if t + 2 < N:
                for side in range(2):
                    og_ring(t + 2, side).start()
            else:
                for side in range(2):
                    in_ring(t - 5, side).start()
        j = t - 7
        if 1 <= j < N:
            for side in range(2):
                in_ring(j, side).wait_recv()
            if j + 2 < N:
                for side in range(2):
                    in_ring(j + 2, side).start()
        if 0 <= t - 2 < N:
            stage_share(t - 2)
        if 1 <= t < N:
            stage_terms(t)
            act_copy(t).wait_recv()
        if 0 <= t - 1 < N:
            stage_act(t - 1)
        if t == N:
            for i in range(1, 4):
                h_copy(i).start()
        if 0 <= t - 3 < N:
            stage_columns(t - 3)
        if 1 <= t < N:
            stage_pair(t)
        if 0 <= t - 2 < N:
            stage_input(t - 2)
        if 0 <= j < N:
            stage_weights(j)
        if t == 12:
            for i in range(1, 4):
                h_copy(i).wait_recv()
            hc_copy().start()
            stage_owner()

    for copy in loads[7:]:
        copy.wait()
    for t in range(1, 15):
        tick(t)

    hc_copy().wait_recv()
    out_down[...] = lax.dot_general(
        hid[...].reshape(N * 2 * ROWS, cols), og_all[...].reshape(N * 2 * ROWS, -1), TN,
        preferred_element_type=F32,
    )
    e_copy().wait_recv()
    out_in[...] = (rbuf[zh].astype(F32) + hrecv[...].astype(F32)).astype(BF)

    for j in range(N):
        t_copy(j).wait_send()
        gc_copy(j).wait_send()
        for i in range(1, 4):
            z_copy(j, i).wait_send()
            g_copy(j, i).wait_send()
            x_copy(j, i).wait_send()
        if j >= 1:
            act_copy(j).wait_send()
            for side in range(2):
                og_ring(j, side).wait_send()
                in_ring(j, side).wait_send()
                f_copy(j, side).wait_send()
    for i in range(1, 4):
        h_copy(i).wait_send()
    hc_copy().wait_send()
    e_copy().wait_send()


def shards(inputs, out_grad, gate_act, up_act, gate_weight, up_weight, down_weight):
    width, cols = gate_weight.shape
    hidden_cols = gate_act.shape[1]
    dma = pltpu.SemaphoreType.DMA
    scratch = [
        pltpu.VMEM((N, 2, ROWS, width), BF),
        pltpu.VMEM((N, 2, ROWS, width), BF),
        pltpu.VMEM((width, cols), BF),
        pltpu.VMEM((width, cols), BF),
        pltpu.VMEM((cols, width), BF),
        pltpu.VMEM((2, 2, SUB, hidden_cols), BF),
        pltpu.VMEM((N, 2, 2, SUB, cols), BF),
        pltpu.VMEM((N, 2, SUB, cols), BF),
        pltpu.VMEM((N, 2, ROWS, cols), BF),
        pltpu.VMEM((N, ROWS, cols), BF),
        pltpu.VMEM((N, 4, SUB, cols), BF),
        pltpu.VMEM((N, 4, SUB, cols), BF),
        pltpu.VMEM((N, 2, 2, 4, SUB, cols), BF),
        pltpu.VMEM((N, 2, 4, SUB, cols), BF),
        pltpu.VMEM((N, 4, 2, ROWS, 128), BF),
        pltpu.VMEM((N, 4, 2, ROWS, 128), BF),
        pltpu.VMEM((N, 2, ROWS, 128), BF),
        pltpu.VMEM((N, 2, ROWS, 128), BF),
        pltpu.VMEM((2, 2 * ROWS, 64), BF),
        pltpu.VMEM((2 * ROWS, 64), BF),
        dma((11,)),
        dma((N, 2)), dma((N, 2)), dma((N, 2)), dma((N, 2)),
        dma((N,)), dma((N,)), dma((N,)), dma((N,)),
        dma((N, 4)), dma((N, 4)), dma((N, 4)), dma((N, 4)),
        dma((N,)), dma((N,)),
        dma((N, 4)), dma((N, 4)),
        dma((N, 2)), dma((N, 2)),
        dma((4,)), dma((4,)), dma((1,)), dma((1,)), dma((1,)), dma((1,)),
    ]
    return pl.pallas_call(
        kernel,
        out_shape=(
            jax.ShapeDtypeStruct((2 * ROWS, 64), BF),
            jax.ShapeDtypeStruct((width, cols), F32),
            jax.ShapeDtypeStruct((width, cols), F32),
            jax.ShapeDtypeStruct((cols, width), F32),
        ),
        in_specs=[pl.BlockSpec(memory_space=pl.ANY)] * 7,
        out_specs=(pl.BlockSpec(memory_space=pltpu.VMEM),) * 4,
        scratch_shapes=scratch,
        compiler_params=pltpu.CompilerParams(
            collective_id=0, has_side_effects=True, vmem_limit_bytes=56 * 1024 * 1024
        ),
        name="swiglu_backward",
    )(out_grad, inputs, gate_act, up_act, gate_weight, up_weight, down_weight)


def solution(mesh):
    in_specs = (
        P("gx", "gy"),
        P("gx", "gy"),
        P("gx", "gz"),
        P("gx", "gz"),
        P("gy", ("gz", "gx")),
        P("gy", ("gz", "gx")),
        P(("gz", "gx"), "gy"),
    )
    out_specs = (
        P("gx", ("gy", "gz")),
        P("gy", ("gz", "gx")),
        P("gy", ("gz", "gx")),
        P(("gz", "gx"), "gy"),
    )
    return jax.shard_map(shards, mesh=mesh, in_specs=in_specs, out_specs=out_specs, check_vma=False)
```

```python
import jax
import jax.numpy as jnp
from jax import lax
from jax.experimental import pallas as pl
from jax.experimental.pallas import tpu as pltpu
from jax.sharding import PartitionSpec as P

MESH = pl.DeviceIdType.MESH
BF = jnp.bfloat16
F32 = jnp.float32
N = 8
ROWS = 128
LAST = N - 1
SUB = 32
NT = (((1,), (1,)), ((), ()))
TN = (((0,), (0,)), ((), ()))
TIMES = (
    (None, 2.7, 5.4, 8.1, 10.8, 13.5, 16.2, 18.9),
    (None, 4.2, 6.9, 9.6, 12.3, 15.0, 17.7, 20.4),
    (5.0, 8.1, 11.2, 14.3, 17.4, 20.5, 23.6, 26.7),
    (9.2, 12.3, 15.4, 18.5, 21.6, 24.7, 27.8, 30.9),
    (11.2, 14.3, 17.4, 20.5, 23.6, 26.7, 29.8, 32.9),
    (15.2, 18.3, 21.4, 24.5, 27.6, 30.7, 33.8, 36.9),
    (None, 21.6, 24.3, 27.0, 29.7, 32.4, 35.1, 37.8),
    (19.0, 21.7, 24.4, 27.1, 29.8, 32.5, 35.2, 37.9),
)
ONCE = (26.8, 36.8, 39.0, 38.8, 44.9)
ACTS_AT = {0: (1,), 1: (2,), 3: (3,), 5: (4, 5), 6: (6,), 7: (7,)}


def kernel(
    og, inp, gact, uact, gw, uw, dw,
    out_in, out_gate, out_up, out_down,
    og_all, inp_all, gw_v, uw_v, dw_v, araw, ast, act,
    tbuf, trecv, sbuf, zrecv, grads, hid, pbuf, xrecv, fbuf, yrecv, ydiag, total_in, rbuf, hrecv,
    load_sem, og_s, og_r, in_s, in_r, act_s, act_r, t_s, t_r, z_s, z_r,
    g_s, g_r, gc_s, gc_r, x_s, x_r, f_s, f_r, h_s, h_r, hc_s, hc_r, e_s, e_r, d_s, d_r,
):
    a, b, c = (lax.axis_index(n) for n in ("gx", "gy", "gz"))
    core, zl = lax.rem(b, 2), lax.div(b, 2)
    x, zh = lax.div(c, 2), lax.rem(c, 2)
    cols = dw.shape[0]

    def y_peer(step):
        return (lax.rem(a + step + N, N), b, c)

    partner = (a, b + 1 - 2 * core, c)
    far = (a, b, c + 1 - 2 * zh)
    diagonal = (lax.rem(a + N // 2, N), b, c + 1 - 2 * zh)
    mine, other = pl.ds(pl.multiple_of(zh * 64, 64), 64), pl.ds(pl.multiple_of(64 - zh * 64, 64), 64)

    def z_peer(i):
        return (a, 2 * lax.rem(zl + i, 4) + core, c)

    def x_peer(i):
        return (a, b, 2 * lax.rem(x + i, 4) + zh)

    def remote(src, dst, s, r, to):
        return pltpu.make_async_remote_copy(
            src_ref=src, dst_ref=dst, send_sem=s, recv_sem=r, device_id=to, device_id_type=MESH
        )

    loads = []
    for h in range(2):
        loads.append((og.at[pl.ds(h * ROWS, ROWS)], og_all.at[0, h]))
    loads.append((dw, dw_v))
    for h in range(2):
        rows = pl.ds(pl.multiple_of(h * ROWS + zl * SUB, SUB), SUB)
        loads.append((gact.at[rows], araw.at[0, h]))
        loads.append((uact.at[rows], araw.at[1, h]))
    loads.append((gw, gw_v))
    loads.append((uw, uw_v))
    for h in range(2):
        loads.append((inp.at[pl.ds(h * ROWS, ROWS)], inp_all.at[0, h]))
    loads = [pltpu.make_async_copy(s, d, load_sem.at[i]) for i, (s, d) in enumerate(loads)]
    for copy in loads:
        copy.start()

    barrier = pltpu.get_barrier_semaphore()
    peers = [y_peer(i) for i in range(1, N)] + [z_peer(i) for i in range(1, 4)]
    peers += [x_peer(i) for i in range(1, 4)] + [partner, far, diagonal]
    for peer in peers:
        pl.semaphore_signal(barrier, inc=1, device_id=peer, device_id_type=MESH)
    pl.semaphore_wait(barrier, len(peers))

    def ring(buf, s, r, m, side):
        src = buf.at[0, (m - 1 + side) % 2] if isinstance(m, int) and m <= 2 else buf.at[m - 2, side]
        return remote(src, buf.at[m, side], s.at[m, side], r.at[m, side], y_peer(1 - 2 * side))

    def og_ring(m, side):
        return ring(og_all, og_s, og_r, m, side)

    def in_ring(m, side):
        return ring(inp_all, in_s, in_r, m, side)

    def act_copy(j):
        to = y_peer((1 - 2 * core) * ((j + 1) // 2))
        return remote(ast.at[to[0], lax.rem(core + j - 1, 2)], act.at[j], act_s.at[j], act_r.at[j], to)

    def t_copy(j):
        return remote(tbuf.at[j, 1 - core], trecv.at[j], t_s.at[j], t_r.at[j], partner)

    def z_copy(j, i):
        to = lax.rem(zl + i, 4)
        return remote(sbuf.at[j, to], zrecv.at[j, zl], z_s.at[j, i], z_r.at[j, i], z_peer(i))

    def g_copy(j, i):
        part = grads.at[j, :, core, zl]
        return remote(part, part, g_s.at[j, i], g_r.at[j, i], z_peer(i))

    def gc_copy(j):
        part = grads.at[j, :, core]
        return remote(part, part, gc_s.at[j], gc_r.at[j], partner)

    def x_copy(j, i):
        to = lax.rem(x + i, 4)
        return remote(pbuf.at[j, to], xrecv.at[j, x], x_s.at[j, i], x_r.at[j, i], x_peer(i))

    def f_copy(j, side):
        step = ((j + 1) // 2) * (2 * side - 1)
        rows = mine if j == LAST else pl.ds(0, 128)
        return remote(
            fbuf.at[j, side, rows], yrecv.at[j, side, rows], f_s.at[j, side], f_r.at[j, side], y_peer(step)
        )

    def d_copy(side):
        return remote(fbuf.at[LAST, side, other], ydiag.at[side], d_s.at[side], d_r.at[side], diagonal)

    def h_copy(i):
        part = hid.at[:, core, zl]
        return remote(part, part, h_s.at[i], h_r.at[i], z_peer(i))

    def hc_copy():
        part = hid.at[:, core]
        return remote(part, part, hc_s.at[0], hc_r.at[0], partner)

    def e_copy():
        return remote(rbuf, hrecv, e_s.at[0], e_r.at[0], far)

    def stage_terms(j):
        term = lax.dot_general(
            og_all[j].reshape(2 * ROWS, -1), dw_v[...], NT, preferred_element_type=F32
        )
        tbuf[j] = term.astype(BF).reshape(2, ROWS, cols)
        t_copy(j).start()

    def stage_pair(j):
        t_copy(j).wait_recv()
        total = tbuf[j, core].astype(F32) + trecv[j].astype(F32)
        sbuf[j] = total.astype(BF).reshape(4, SUB, cols)
        for i in range(1, 4):
            z_copy(j, i).start()

    def stage_act(j):
        for i in range(1, 4):
            z_copy(j, i).wait_recv()
        own = sbuf[j, zl]
        zrecv[j, zl] = own
        hidden_grad = zrecv[j, 0].astype(F32)
        for i in range(1, 4):
            hidden_grad += zrecv[j, i].astype(F32)
        gate, up = act[j, 0].astype(F32), act[j, 1].astype(F32)
        sigma = jax.nn.sigmoid(gate)
        silu = gate * sigma
        grads[j, 0, core, zl] = (hidden_grad * up * sigma * (1.0 + gate * (1.0 - sigma))).astype(BF)
        grads[j, 1, core, zl] = (hidden_grad * silu).astype(BF)
        hid[j, core, zl] = (silu * up).astype(BF)
        for i in range(1, 4):
            g_copy(j, i).start()

    def stage_share(j):
        for i in range(1, 4):
            g_copy(j, i).wait_recv()
        gc_copy(j).start()

    def stage_input(j):
        gc_copy(j).wait_recv()
        part = jnp.dot(
            grads[j, 0].reshape(2 * ROWS, cols), gw_v[...], preferred_element_type=F32
        ) + jnp.dot(grads[j, 1].reshape(2 * ROWS, cols), uw_v[...], preferred_element_type=F32)
        for i in range(4):
            pbuf[j, i] = part[:, i * 128:(i + 1) * 128].astype(BF).reshape(2, ROWS, 128)
        for i in range(1, 4):
            x_copy(j, i).start()

    def stage_columns(j):
        for i in range(1, 4):
            x_copy(j, i).wait_recv()
        xrecv[j, x] = pbuf[j, x]
        total = xrecv[j, 0].astype(F32)
        for i in range(1, 4):
            total += xrecv[j, i].astype(F32)
        for side in range(2):
            if j == 0:
                yrecv[0, side] = total[side].T.astype(BF)
            else:
                fbuf[j, side] = total[side].T.astype(BF)
                f_copy(j, side).start()
                if j == LAST:
                    d_copy(side).start()

    def stage_weights(j):
        block = inp_all[j].reshape(2 * ROWS, -1)
        gate = lax.dot_general(grads[j, 0].reshape(2 * ROWS, cols), block, TN, preferred_element_type=F32)
        up = lax.dot_general(grads[j, 1].reshape(2 * ROWS, cols), block, TN, preferred_element_type=F32)
        if isinstance(j, int) and j == 0:
            out_gate[...] = gate
            out_up[...] = up
        else:
            out_gate[...] += gate
            out_up[...] += up

    def stage_owner():
        for j in range(1, LAST):
            for side in range(2):
                f_copy(j, side).wait_recv()
        for half in range(2):
            total = yrecv[0, half].astype(F32)
            for j in range(1, LAST):
                total += yrecv[j, (j - 1 + half) % 2].astype(F32)
            total_in[:, half * ROWS:(half + 1) * ROWS] = total
        rbuf[...] = total_in[other].astype(BF)
        e_copy().start()

    def stage_result():
        e_copy().wait_recv()
        for half in range(2):
            f_copy(LAST, half).wait_recv()
            d_copy(half).wait_recv()
        for half in range(2):
            cut = slice(half * ROWS, (half + 1) * ROWS)
            total = total_in[mine, cut] + hrecv[:, cut].astype(F32)
            total += yrecv[LAST, half, mine].astype(F32) + ydiag[half].astype(F32)
            out_in[:, cut] = total.astype(BF)

    def stage_down():
        hc_copy().wait_recv()
        out_down[...] = lax.dot_general(
            hid[...].reshape(N * 2 * ROWS, cols), og_all[...].reshape(N * 2 * ROWS, -1), TN,
            preferred_element_type=F32,
        )

    for i in range(3):
        loads[i].wait()
    for m in (1, 2):
        for side in range(2):
            og_ring(m, side).start()
    stage_terms(0)
    for i in range(3, 7):
        loads[i].wait()
    for kind in range(2):
        for h in range(2):
            block = araw[kind, h]
            for i in range(N):
                ast[i, h, kind] = block[:, i * cols:(i + 1) * cols]
    act[0] = ast[a, core]
    for j in ACTS_AT[0]:
        act_copy(j).start()
    stage_pair(0)

    for copy in loads[7:]:
        copy.wait()

    steps = []

    def og_step(j):
        for side in range(2):
            og_ring(j, side).wait_recv()
        for side in range(2):
            if j + 2 < N:
                og_ring(j + 2, side).start()
            else:
                in_ring(j - 5, side).start()
        for i in ACTS_AT.get(j, ()):
            act_copy(i).start()
        stage_terms(j)

    def in_step(j):
        for side in range(2):
            in_ring(j, side).wait_recv()
        if j + 2 < N:
            for side in range(2):
                in_ring(j + 2, side).start()

    def act_step(j):
        if j:
            act_copy(j).wait_recv()
        stage_act(j)

    def hid_start():
        for i in range(1, 4):
            h_copy(i).start()

    def hid_share():
        for i in range(1, 4):
            h_copy(i).wait_recv()
        hc_copy().start()

    stages = (og_step, stage_pair, act_step, stage_share, stage_input, stage_columns, in_step, stage_weights)
    for stage, times in zip(stages, TIMES, strict=True):
        steps += [(when, stage, (j,)) for j, when in enumerate(times) if when is not None]
    once = (hid_start, hid_share, stage_down, stage_owner, stage_result)
    steps += [(when, step, ()) for step, when in zip(once, ONCE, strict=True)]
    for _, step, args in sorted(steps, key=lambda s: s[0]):
        step(*args)

    for j in range(N):
        t_copy(j).wait_send()
        gc_copy(j).wait_send()
        for i in range(1, 4):
            z_copy(j, i).wait_send()
            g_copy(j, i).wait_send()
            x_copy(j, i).wait_send()
        if j >= 1:
            act_copy(j).wait_send()
            for side in range(2):
                og_ring(j, side).wait_send()
                in_ring(j, side).wait_send()
                f_copy(j, side).wait_send()
    for i in range(1, 4):
        h_copy(i).wait_send()
    hc_copy().wait_send()
    e_copy().wait_send()
    for side in range(2):
        d_copy(side).wait_send()


def deliver(*refs):
    arrays, results, held, sems = refs[0:4], refs[4:8], refs[8:12], refs[12]
    fetch = [pltpu.make_async_copy(arrays[i], held[i], sems.at[0, i]) for i in range(4)]
    store = [pltpu.make_async_copy(held[i], results[i], sems.at[1, i]) for i in range(4)]
    for copy in fetch:
        copy.start()
    for i in range(4):
        fetch[i].wait()
        store[i].start()
    for copy in store:
        copy.wait()


def shards(inputs, out_grad, gate_act, up_act, gate_weight, up_weight, down_weight):
    width, cols = gate_weight.shape
    hidden_cols = gate_act.shape[1]
    dma = pltpu.SemaphoreType.DMA
    scratch = [
        pltpu.VMEM((N, 2, ROWS, width), BF),
        pltpu.VMEM((N, 2, ROWS, width), BF),
        pltpu.VMEM((cols, width), BF),
        pltpu.VMEM((cols, width), BF),
        pltpu.VMEM((cols, width), BF),
        pltpu.VMEM((2, 2, SUB, hidden_cols), BF),
        pltpu.VMEM((N, 2, 2, SUB, cols), BF),
        pltpu.VMEM((N, 2, SUB, cols), BF),
        pltpu.VMEM((N, 2, ROWS, cols), BF),
        pltpu.VMEM((N, ROWS, cols), BF),
        pltpu.VMEM((N, 4, SUB, cols), BF),
        pltpu.VMEM((N, 4, SUB, cols), BF),
        pltpu.VMEM((N, 2, 2, 4, SUB, cols), BF),
        pltpu.VMEM((N, 2, 4, SUB, cols), BF),
        pltpu.VMEM((N, 4, 2, ROWS, 128), BF),
        pltpu.VMEM((N, 4, 2, ROWS, 128), BF),
        pltpu.VMEM((N, 2, ROWS, 128), BF),
        pltpu.VMEM((N, 2, ROWS, 128), BF),
        pltpu.VMEM((2, 64, ROWS), BF),
        pltpu.VMEM((128, 2 * ROWS), F32),
        pltpu.VMEM((64, 2 * ROWS), BF),
        pltpu.VMEM((64, 2 * ROWS), BF),
        dma((11,)),
        dma((N, 2)), dma((N, 2)), dma((N, 2)), dma((N, 2)),
        dma((N,)), dma((N,)), dma((N,)), dma((N,)),
        dma((N, 4)), dma((N, 4)), dma((N, 4)), dma((N, 4)),
        dma((N,)), dma((N,)),
        dma((N, 4)), dma((N, 4)),
        dma((N, 2)), dma((N, 2)),
        dma((4,)), dma((4,)), dma((1,)), dma((1,)), dma((1,)), dma((1,)), dma((2,)), dma((2,)),
    ]
    results = pl.pallas_call(
        kernel,
        out_shape=(
            jax.ShapeDtypeStruct((64, 2 * ROWS), BF),
            jax.ShapeDtypeStruct((cols, width), F32),
            jax.ShapeDtypeStruct((cols, width), F32),
            jax.ShapeDtypeStruct((cols, width), F32),
        ),
        in_specs=[pl.BlockSpec(memory_space=pl.ANY)] * 7,
        out_specs=(pl.BlockSpec(memory_space=pltpu.VMEM),) * 4,
        scratch_shapes=scratch,
        compiler_params=pltpu.CompilerParams(
            collective_id=0, has_side_effects=True, vmem_limit_bytes=56 * 1024 * 1024
        ),
        name="swiglu_backward",
    )(out_grad, inputs, gate_act, up_act, gate_weight.T, up_weight.T, down_weight)
    input_grad, gate_grad, up_grad, down_grad = pl.pallas_call(
        deliver,
        out_shape=tuple(jax.ShapeDtypeStruct(r.shape, r.dtype) for r in results),
        in_specs=[pl.BlockSpec(memory_space=pl.ANY)] * 4,
        out_specs=(pl.BlockSpec(memory_space=pl.ANY),) * 4,
        scratch_shapes=[pltpu.VMEM(r.shape, r.dtype) for r in results] + [dma((2, 4))],
        name="deliver",
    )(*results)
    return (input_grad.T, gate_grad.T, up_grad.T, down_grad)


def solution(mesh):
    in_specs = (
        P("gx", "gy"),
        P("gx", "gy"),
        P("gx", "gz"),
        P("gx", "gz"),
        P("gy", ("gz", "gx")),
        P("gy", ("gz", "gx")),
        P(("gz", "gx"), "gy"),
    )
    out_specs = (
        P("gx", ("gy", "gz")),
        P("gy", ("gz", "gx")),
        P("gy", ("gz", "gx")),
        P(("gz", "gx"), "gy"),
    )
    return jax.shard_map(shards, mesh=mesh, in_specs=in_specs, out_specs=out_specs, check_vma=False)
```

```python
import jax
import jax.numpy as jnp
from jax import lax
from jax.experimental import pallas as pl
from jax.experimental.pallas import tpu as pltpu
from jax.sharding import PartitionSpec as P

MESH = pl.DeviceIdType.MESH
BF = jnp.bfloat16
F32 = jnp.float32
N = 8
ROWS = 128
LAST = N - 1
FULL = 1
SUB = 32
NT = (((1,), (1,)), ((), ()))
TN = (((0,), (0,)), ((), ()))
TIMES = (
    (None, 8.60, 11.45, 16.18, 19.26, 24.23, 28.05, 33.09),
    (9.84, 13.94, 16.79, 22.06, 26.24, 30.41, 34.98, 38.93),
    (15.68, 21.02, 25.37, 29.37, 33.69, 37.72, 42.06, 46.01),
    (24.77, 27.55, 35.90, 38.68, 41.46, 44.24, 48.25, 52.19),
    (4.80, 13.02, 21.32, 46.31, 50.09),
    (17.98, 28.25, 36.10, 58.15, 60.34),
)
ONCE = (39.03, 55.25, 57.95, 54.58, 61.78)
ACTS_AT = {0: (1,), 1: (2,), 2: (3,), 3: (4,), 4: (5,), 5: (6, 7)}


def kernel(
    og, inp, gact, uact, gw, uw, dw,
    out_in, out_gate, out_up, out_down,
    og_all, og_far, inp_all, gw_v, uw_v, dw_v, araw, ast, act,
    sbuf, zrecv, whole, grads, hid, pbuf, xrecv, fbuf, yrecv, ydiag, total_in, rbuf, hrecv,
    load_sem, swap_s, swap_r, og_s, og_r, oc_s, oc_r, in_s, in_r, ix_s, ix_r, act_s, act_r, z_s, z_r,
    g_s, g_r, gc_s, gc_r, x_s, x_r, f_s, f_r, h_s, h_r, hc_s, hc_r, e_s, e_r, d_s, d_r,
):
    a, b, c = (lax.axis_index(n) for n in ("gx", "gy", "gz"))
    core, zl = lax.rem(b, 2), lax.div(b, 2)
    x, zh = lax.div(c, 2), lax.rem(c, 2)
    cols = dw.shape[0]

    def y_peer(step):
        return (lax.rem(a + step + N, N), b, c)

    partner = (a, b + 1 - 2 * core, c)
    far = (a, b, c + 1 - 2 * zh)
    diagonal = (lax.rem(a + N // 2, N), b, c + 1 - 2 * zh)
    mine, other = pl.ds(pl.multiple_of(zh * 64, 64), 64), pl.ds(pl.multiple_of(64 - zh * 64, 64), 64)

    def z_peer(i):
        return (a, 2 * lax.rem(zl + i, 4) + core, c)

    def x_peer(i, to_core):
        return (a, 2 * zl + to_core, 2 * lax.rem(x + i, 4) + zh)

    def remote(src, dst, s, r, to):
        return pltpu.make_async_remote_copy(
            src_ref=src, dst_ref=dst, send_sem=s, recv_sem=r, device_id=to, device_id_type=MESH
        )

    loads = []
    for h in range(2):
        loads.append((og.at[pl.ds(h * ROWS, ROWS)], og_all.at[h, core]))
    for array, held in ((dw, dw_v), (gw, gw_v), (uw, uw_v)):
        loads.append((array, held.at[core]))
    for h in range(2):
        rows = pl.ds(h * ROWS, ROWS)
        loads.append((gact.at[rows], araw.at[0, h]))
        loads.append((uact.at[rows], araw.at[1, h]))
    for h in range(2):
        for q in range(2):
            loads.append((inp.at[pl.ds(h * ROWS + q * 64, 64)], inp_all.at[0, 2 * h + q]))
    loads = [pltpu.make_async_copy(s, d, load_sem.at[i]) for i, (s, d) in enumerate(loads)]
    for copy in loads:
        copy.start()

    barrier = pltpu.get_barrier_semaphore()
    peers = [y_peer(i) for i in range(1, N)] + [z_peer(i) for i in range(1, 4)]
    peers += [x_peer(i, k) for i in range(1, 4) for k in (core, 1 - core)] + [partner, far, diagonal]
    for peer in peers:
        pl.semaphore_signal(barrier, inc=1, device_id=peer, device_id_type=MESH)
    pl.semaphore_wait(barrier, len(peers))

    swaps = [og_all.at[1 - core, core], og_all.at[core, core], dw_v.at[core], gw_v.at[core], uw_v.at[core]]
    swaps = [remote(part, part, swap_s.at[i], swap_r.at[i], partner) for i, part in enumerate(swaps)]

    def half(m):
        return lax.rem(m - 1 + core, 2)

    def place(j):
        return core if j == 0 else j + 1

    def og_ring(m, k):
        src = og_all.at[half(m), k] if m <= 2 else og_all.at[m - 1, k]
        return remote(src, og_all.at[m + 1, k], og_s.at[m, k], og_r.at[m, k], y_peer(1 - 2 * core))

    def oc_copy(j):
        return remote(og_all.at[place(j), 1 - core], og_far.at[j], oc_s.at[j], oc_r.at[j], partner)

    def in_ring(d, side):
        src, dst = (d - 1, d) if side == 0 else ((N + 1 - d) % N, N - d)
        rows = pl.ds(0, 64) if d < 4 else pl.ds(32 * side, 32)
        return remote(
            inp_all.at[src, x, rows], inp_all.at[dst, x, rows], in_s.at[d, side], in_r.at[d, side],
            y_peer(1 - 2 * side),
        )

    def ix_copy(rel, i):
        part = inp_all.at[rel, x]
        return remote(part, part, ix_s.at[rel, i], ix_r.at[rel, i], x_peer(i, core))

    own_rows = pl.ds(pl.multiple_of(zl * SUB, SUB), SUB)

    def act_copy(j):
        to = y_peer((1 - 2 * core) * ((j + 1) // 2))
        rows = pl.ds(0, ROWS) if j < FULL else own_rows
        return remote(ast.at[to[0], half(j), :, rows], act.at[j, :, rows], act_s.at[j], act_r.at[j], to)

    def z_copy(j, i):
        to = lax.rem(zl + i, 4)
        return remote(sbuf.at[j, to], zrecv.at[j, zl], z_s.at[j, i], z_r.at[j, i], z_peer(i))

    def g_copy(j, i):
        part = whole.at[j, zl] if j < FULL else grads.at[j, :, core, zl]
        return remote(part, part, g_s.at[j, i], g_r.at[j, i], z_peer(i))

    def gc_copy(j):
        part = grads.at[j, :, core]
        return remote(part, part, gc_s.at[j], gc_r.at[j], partner)

    def x_copy(j, i, k):
        to, to_core = lax.rem(x + i, 4), core + k * (1 - 2 * core)
        return remote(
            pbuf.at[j, to_core, to], xrecv.at[j, x, core], x_s.at[j, i, k], x_r.at[j, i, k], x_peer(i, to_core)
        )

    def f_copy(j, side):
        step = ((j + 1) // 2) * (2 * side - 1)
        rows = mine if j == LAST else pl.ds(0, 128)
        return remote(
            fbuf.at[j, side, rows], yrecv.at[j, side, rows], f_s.at[j, side], f_r.at[j, side], y_peer(step)
        )

    def d_copy(side):
        return remote(fbuf.at[LAST, side, other], ydiag.at[side], d_s.at[side], d_r.at[side], diagonal)

    def h_copy(i):
        part = hid.at[pl.ds(FULL, N - FULL), core, zl]
        return remote(part, part, h_s.at[i], h_r.at[i], z_peer(i))

    def hc_copy():
        part = hid.at[:, core]
        return remote(part, part, hc_s.at[0], hc_r.at[0], partner)

    def e_copy():
        return remote(rbuf, hrecv, e_s.at[0], e_r.at[0], far)

    def stage_terms(j):
        term = sum(
            lax.dot_general(og_all[place(j), k], dw_v[k], NT, preferred_element_type=F32) for k in range(2)
        )
        sbuf[j] = term.astype(BF).reshape(4, SUB, cols)
        for i in range(1, 4):
            z_copy(j, i).start()
        oc_copy(j).start()

    def derive(hidden_grad, gate, up):
        sigma = jax.nn.sigmoid(gate)
        silu = gate * sigma
        gate_grad = hidden_grad * up * sigma * (1.0 + gate * (1.0 - sigma))
        return [v.astype(BF) for v in (gate_grad, hidden_grad * silu, silu * up)]

    def stage_act(j):
        for i in range(1, 4):
            z_copy(j, i).wait_recv()
        zrecv[j, zl] = sbuf[j, zl]
        hidden_grad = zrecv[j, 0].astype(F32)
        for i in range(1, 4):
            hidden_grad += zrecv[j, i].astype(F32)
        if j < FULL:
            whole[j, zl] = hidden_grad.astype(BF)
        else:
            gate, up = act[j, 0, own_rows].astype(F32), act[j, 1, own_rows].astype(F32)
            grads[j, 0, core, zl], grads[j, 1, core, zl], hid[j, core, zl] = derive(hidden_grad, gate, up)
        for i in range(1, 4):
            g_copy(j, i).start()

    def stage_input(j):
        for i in range(1, 4):
            g_copy(j, i).wait_recv()
        if j == 0:
            swaps[3].wait_recv()
            swaps[4].wait_recv()
        if j < FULL:
            gate, up = act[j, 0].astype(F32), act[j, 1].astype(F32)
            block = (4, SUB, cols)
            values = derive(whole[j].reshape(ROWS, cols).astype(F32), gate, up)
            grads[j, 0, core], grads[j, 1, core], hid[j, core] = [v.reshape(block) for v in values]
        gate, up = grads[j, 0, core].reshape(ROWS, cols), grads[j, 1, core].reshape(ROWS, cols)
        for k in range(2):
            part = jnp.dot(gate, gw_v[k], preferred_element_type=F32)
            part += jnp.dot(up, uw_v[k], preferred_element_type=F32)
            for i in range(4):
                pbuf[j, k, i] = part[:, i * 128:(i + 1) * 128].astype(BF)
        for i in range(1, 4):
            for k in range(2):
                x_copy(j, i, k).start()
        x_copy(j, 0, 1).start()
        gc_copy(j).start()

    def stage_columns(j):
        x_copy(j, 0, 1).wait_recv()
        for i in range(1, 4):
            for k in range(2):
                x_copy(j, i, k).wait_recv()
        xrecv[j, x, core] = pbuf[j, core, x]
        total = xrecv[j, 0].astype(F32)
        for i in range(1, 4):
            total += xrecv[j, i].astype(F32)
        for side in range(2):
            if j == 0:
                yrecv[0, side] = total[side].T.astype(BF)
            else:
                fbuf[j, side] = total[side].T.astype(BF)
                f_copy(j, side).start()
                if j == LAST:
                    d_copy(side).start()

    def stage_weights(d):
        for j in sorted({max(2 * d - 1, 0), min(2 * d, LAST)}):
            gc_copy(j).wait_recv()
        for rel in sorted({d, (N - d) % N}):
            if rel:
                for i in range(1, 4):
                    ix_copy(rel, i).wait_recv()
            if rel in (0, 4):
                halves = ((max(2 * d - 1, 0), 0), (max(2 * d - 1, 0), 1))
            elif rel < 4:
                halves = ((2 * d - 1, 0), (2 * d, 0))
            else:
                halves = ((2 * d, 1), (2 * d - 1, 1))
            block = inp_all[rel].reshape(2 * ROWS, -1)
            for kind, out in enumerate((out_gate, out_up)):
                part = jnp.concatenate([grads[j, kind, side].reshape(ROWS, cols) for j, side in halves])
                term = lax.dot_general(part, block, TN, preferred_element_type=F32)
                out[...] = out[...] + term if rel else term

    def stage_owner():
        for j in range(1, LAST):
            for side in range(2):
                f_copy(j, side).wait_recv()
        for half in range(2):
            total = yrecv[0, half].astype(F32)
            for j in range(1, LAST):
                total += yrecv[j, (j - 1 + half) % 2].astype(F32)
            total_in[:, half * ROWS:(half + 1) * ROWS] = total
        rbuf[...] = total_in[other].astype(BF)
        e_copy().start()

    def stage_result():
        e_copy().wait_recv()
        for half in range(2):
            f_copy(LAST, half).wait_recv()
            d_copy(half).wait_recv()
        for half in range(2):
            cut = slice(half * ROWS, (half + 1) * ROWS)
            total = total_in[mine, cut] + hrecv[:, cut].astype(F32)
            total += yrecv[LAST, half, mine].astype(F32) + ydiag[half].astype(F32)
            out_in[:, cut] = total.astype(BF)

    def stage_down():
        hc_copy().wait_recv()
        for j in range(N):
            oc_copy(j).wait_recv()
        near = jnp.concatenate([og_all[place(j), core] for j in range(N)])
        far_block = og_far[...].reshape(N * ROWS, -1)
        total = lax.dot_general(
            hid[:, core].reshape(N * ROWS, cols), near, TN, preferred_element_type=F32
        ) + lax.dot_general(
            hid[:, 1 - core].reshape(N * ROWS, cols), far_block, TN, preferred_element_type=F32
        )
        out_down[...] = total

    loads[0].wait()
    loads[1].wait()
    swaps[0].start()
    og_ring(1, core).start()
    swaps[1].start()
    og_ring(2, core).start()
    for load, swap in zip(loads[2:5], swaps[2:]):
        load.wait()
        swap.start()
    swaps[0].wait_recv()
    og_ring(1, 1 - core).start()
    swaps[1].wait_recv()
    og_ring(2, 1 - core).start()
    swaps[2].wait_recv()
    stage_terms(0)
    for i in range(5, 9):
        loads[i].wait()
    for h in range(2):
        for kind in range(2):
            block = araw[kind, h]
            for i in range(N):
                ast[i, h, kind] = block[:, i * cols:(i + 1) * cols]
    act[0] = ast[a, core]
    for j in ACTS_AT[0]:
        act_copy(j).start()
    for copy in loads[9:]:
        copy.wait()

    steps = []

    def og_step(j):
        for k in range(2):
            og_ring(j, k).wait_recv()
        for k in range(2):
            if j + 2 < N:
                og_ring(j + 2, k).start()
        for i in ACTS_AT.get(j, ()):
            act_copy(i).start()
        stage_terms(j)

    def in_step(d):
        if d:
            for side in range(2):
                in_ring(d, side).wait_recv()
        if d < 4:
            for side in range(2):
                in_ring(d + 1, side).start()
        for rel in sorted({d, (N - d) % N} - {0}):
            for i in range(1, 4):
                ix_copy(rel, i).start()

    def act_step(j):
        if j:
            act_copy(j).wait_recv()
        stage_act(j)

    def hid_start():
        for i in range(1, 4):
            h_copy(i).start()

    def hid_share():
        for i in range(1, 4):
            h_copy(i).wait_recv()
        hc_copy().start()

    stages = (og_step, act_step, stage_input, stage_columns, in_step, stage_weights)
    for stage, times in zip(stages, TIMES, strict=True):
        steps += [(when, stage, (j,)) for j, when in enumerate(times) if when is not None]
    once = (hid_start, hid_share, stage_down, stage_owner, stage_result)
    steps += [(when, step, ()) for step, when in zip(once, ONCE, strict=True)]
    for _, step, args in sorted(steps, key=lambda s: s[0]):
        step(*args)

    for j in range(N):
        oc_copy(j).wait_send()
        gc_copy(j).wait_send()
        x_copy(j, 0, 1).wait_send()
        for i in range(1, 4):
            z_copy(j, i).wait_send()
            g_copy(j, i).wait_send()
            for k in range(2):
                x_copy(j, i, k).wait_send()
        if j >= 1:
            act_copy(j).wait_send()
            for side in range(2):
                og_ring(j, side).wait_send()
                f_copy(j, side).wait_send()
    for i in range(1, 4):
        h_copy(i).wait_send()
    for swap in swaps:
        swap.wait_send()
    hc_copy().wait_send()
    e_copy().wait_send()
    for side in range(2):
        d_copy(side).wait_send()
        for d in range(1, 5):
            in_ring(d, side).wait_send()
    for rel in range(1, N):
        for i in range(1, 4):
            ix_copy(rel, i).wait_send()


def deliver(*refs):
    arrays, results, held, sems = refs[0:4], refs[4:8], refs[8:12], refs[12]
    fetch = [pltpu.make_async_copy(arrays[i], held[i], sems.at[0, i]) for i in range(4)]
    store = [pltpu.make_async_copy(held[i], results[i], sems.at[1, i]) for i in range(4)]
    for copy in fetch:
        copy.start()
    for i in range(4):
        fetch[i].wait()
        store[i].start()
    for copy in store:
        copy.wait()


def shards(inputs, out_grad, gate_act, up_act, gate_weight, up_weight, down_weight):
    width, cols = gate_weight.shape
    hidden_cols = gate_act.shape[1]
    dma = pltpu.SemaphoreType.DMA
    scratch = [
        pltpu.VMEM((N + 1, 2, ROWS, width), BF),
        pltpu.VMEM((N, ROWS, width), BF),
        pltpu.VMEM((N, 4, ROWS // 2, width), BF),
        pltpu.VMEM((2, cols, width), BF),
        pltpu.VMEM((2, cols, width), BF),
        pltpu.VMEM((2, cols, width), BF),
        pltpu.VMEM((2, 2, ROWS, hidden_cols), BF),
        pltpu.VMEM((N, 2, 2, ROWS, cols), BF),
        pltpu.VMEM((N, 2, ROWS, cols), BF),
        pltpu.VMEM((N, 4, SUB, cols), BF),
        pltpu.VMEM((N, 4, SUB, cols), BF),
        pltpu.VMEM((N, 4, SUB, cols), BF),
        pltpu.VMEM((N, 2, 2, 4, SUB, cols), BF),
        pltpu.VMEM((N, 2, 4, SUB, cols), BF),
        pltpu.VMEM((N, 2, 4, ROWS, 128), BF),
        pltpu.VMEM((N, 4, 2, ROWS, 128), BF),
        pltpu.VMEM((N, 2, ROWS, 128), BF),
        pltpu.VMEM((N, 2, ROWS, 128), BF),
        pltpu.VMEM((2, 64, ROWS), BF),
        pltpu.VMEM((128, 2 * ROWS), F32),
        pltpu.VMEM((64, 2 * ROWS), BF),
        pltpu.VMEM((64, 2 * ROWS), BF),
        dma((13,)), dma((5,)), dma((5,)),
        dma((N, 2)), dma((N, 2)), dma((N,)), dma((N,)), dma((5, 2)), dma((5, 2)), dma((N, 4)), dma((N, 4)),
        dma((N,)), dma((N,)),
        dma((N, 4)), dma((N, 4)), dma((N, 4)), dma((N, 4)),
        dma((N,)), dma((N,)),
        dma((N, 4, 2)), dma((N, 4, 2)),
        dma((N, 2)), dma((N, 2)),
        dma((4,)), dma((4,)), dma((1,)), dma((1,)), dma((1,)), dma((1,)), dma((2,)), dma((2,)),
    ]
    results = pl.pallas_call(
        kernel,
        out_shape=(
            jax.ShapeDtypeStruct((64, 2 * ROWS), BF),
            jax.ShapeDtypeStruct((cols, width), F32),
            jax.ShapeDtypeStruct((cols, width), F32),
            jax.ShapeDtypeStruct((cols, width), F32),
        ),
        in_specs=[pl.BlockSpec(memory_space=pl.ANY)] * 7,
        out_specs=(pl.BlockSpec(memory_space=pltpu.VMEM),) * 4,
        scratch_shapes=scratch,
        compiler_params=pltpu.CompilerParams(
            collective_id=0, has_side_effects=True, vmem_limit_bytes=56 * 1024 * 1024
        ),
        name="swiglu_backward",
    )(out_grad, inputs, gate_act, up_act, gate_weight.T, up_weight.T, down_weight)
    input_grad, gate_grad, up_grad, down_grad = pl.pallas_call(
        deliver,
        out_shape=tuple(jax.ShapeDtypeStruct(r.shape, r.dtype) for r in results),
        in_specs=[pl.BlockSpec(memory_space=pl.ANY)] * 4,
        out_specs=(pl.BlockSpec(memory_space=pl.ANY),) * 4,
        scratch_shapes=[pltpu.VMEM(r.shape, r.dtype) for r in results] + [dma((2, 4))],
        name="deliver",
    )(*results)
    return (input_grad.T, gate_grad.T, up_grad.T, down_grad)


def solution(mesh):
    in_specs = (
        P("gx", "gy"),
        P("gx", "gy"),
        P("gx", "gz"),
        P("gx", "gz"),
        P("gy", ("gz", "gx")),
        P("gy", ("gz", "gx")),
        P(("gz", "gx"), "gy"),
    )
    out_specs = (
        P("gx", ("gy", "gz")),
        P("gy", ("gz", "gx")),
        P("gy", ("gz", "gx")),
        P(("gz", "gx"), "gy"),
    )
    return jax.shard_map(shards, mesh=mesh, in_specs=in_specs, out_specs=out_specs, check_vma=False)
```

```python
import jax
import jax.numpy as jnp
from jax import lax
from jax.experimental import pallas as pl
from jax.experimental.pallas import tpu as pltpu
from jax.sharding import PartitionSpec as P

MESH = pl.DeviceIdType.MESH
BF = jnp.bfloat16
F32 = jnp.float32
N = 8
ROWS = 128
LAST = N - 1
FULL = 1
SUB = 32
NT = (((1,), (1,)), ((), ()))
TN = (((0,), (0,)), ((), ()))
TIMES = (
    (None, 8.90, 11.75, 16.48, 19.56, 24.53, 28.35, 33.39),
    (9.84, 14.24, 17.09, 22.36, 26.54, 30.71, 35.28, 39.23),
    (15.98, 21.32, 25.67, 29.67, 33.99, 38.02, 42.36, 46.31),
    (25.07, 27.85, 36.20, 38.98, 41.76, 44.54, 48.55, 52.49),
    (4.80, 13.32, 21.62, 46.61, 50.69),
    (18.28, 28.55, 36.40, 58.45, 60.64),
)
ONCE = (39.33, 55.55, 58.25, 55.18, 62.38)
ACTS_AT = {0: (1,), 1: (2,), 2: (3,), 3: (4,), 4: (5,), 5: (6,), 6: (7,)}


def kernel(
    og, inp, gact, uact, gw, uw, dw,
    out_in, out_gate, out_up, out_down,
    og_all, og_far, inp_all, gw_v, uw_v, dw_v, araw, ast, act,
    sbuf, zrecv, whole, grads, hid, pbuf, xrecv, fbuf, yrecv, ydiag, total_in, rbuf, hrecv,
    load_sem, swap_s, swap_r, og_s, og_r, oc_s, oc_r, in_s, in_r, ix_s, ix_r, act_s, act_r, z_s, z_r,
    g_s, g_r, gc_s, gc_r, x_s, x_r, f_s, f_r, h_s, h_r, hc_s, hc_r, e_s, e_r, d_s, d_r,
):
    a, b, c = (lax.axis_index(n) for n in ("gx", "gy", "gz"))
    core, zl = lax.rem(b, 2), lax.div(b, 2)
    x, zh = lax.div(c, 2), lax.rem(c, 2)
    cols = dw.shape[0]

    def y_peer(step):
        return (lax.rem(a + step + N, N), b, c)

    partner = (a, b + 1 - 2 * core, c)
    far = (a, b, c + 1 - 2 * zh)
    diagonal = (lax.rem(a + N // 2, N), b, c + 1 - 2 * zh)
    mine, other = pl.ds(pl.multiple_of(zh * 64, 64), 64), pl.ds(pl.multiple_of(64 - zh * 64, 64), 64)

    def z_peer(i):
        return (a, 2 * lax.rem(zl + i, 4) + core, c)

    def x_peer(i, to_core):
        return (a, 2 * zl + to_core, 2 * lax.rem(x + i, 4) + zh)

    def remote(src, dst, s, r, to):
        return pltpu.make_async_remote_copy(
            src_ref=src, dst_ref=dst, send_sem=s, recv_sem=r, device_id=to, device_id_type=MESH
        )

    loads = []
    for h in range(2):
        loads.append((og.at[pl.ds(h * ROWS, ROWS)], og_all.at[h, core]))
    for array, held in ((dw, dw_v), (gw, gw_v), (uw, uw_v)):
        loads.append((array, held.at[core]))
    for h in range(2):
        rows = pl.ds(h * ROWS, ROWS)
        loads.append((gact.at[rows], araw.at[0, h]))
        loads.append((uact.at[rows], araw.at[1, h]))
    for h in range(2):
        for q in range(2):
            loads.append((inp.at[pl.ds(h * ROWS + q * 64, 64)], inp_all.at[0, 2 * h + q]))
    loads = [pltpu.make_async_copy(s, d, load_sem.at[i]) for i, (s, d) in enumerate(loads)]
    for copy in loads:
        copy.start()

    barrier = pltpu.get_barrier_semaphore()
    peers = [y_peer(i) for i in range(1, N)] + [z_peer(i) for i in range(1, 4)]
    peers += [x_peer(i, k) for i in range(1, 4) for k in (core, 1 - core)] + [partner, far, diagonal]
    for peer in peers:
        pl.semaphore_signal(barrier, inc=1, device_id=peer, device_id_type=MESH)
    pl.semaphore_wait(barrier, len(peers))

    swaps = [og_all.at[1 - core, core], og_all.at[core, core], dw_v.at[core], gw_v.at[core], uw_v.at[core]]
    swaps = [remote(part, part, swap_s.at[i], swap_r.at[i], partner) for i, part in enumerate(swaps)]

    def half(m):
        return lax.rem(m - 1 + core, 2)

    def place(j):
        return core if j == 0 else j + 1

    def og_ring(m, k):
        src = og_all.at[half(m), k] if m <= 2 else og_all.at[m - 1, k]
        return remote(src, og_all.at[m + 1, k], og_s.at[m, k], og_r.at[m, k], y_peer(1 - 2 * core))

    def oc_copy(j):
        return remote(og_all.at[place(j), 1 - core], og_far.at[j], oc_s.at[j], oc_r.at[j], partner)

    def in_ring(d, side):
        src, dst = (d - 1, d) if side == 0 else ((N + 1 - d) % N, N - d)
        rows = pl.ds(0, 64) if d < 4 else pl.ds(32 * side, 32)
        return remote(
            inp_all.at[src, x, rows], inp_all.at[dst, x, rows], in_s.at[d, side], in_r.at[d, side],
            y_peer(1 - 2 * side),
        )

    def ix_copy(rel, i):
        part = inp_all.at[rel, x]
        return remote(part, part, ix_s.at[rel, i], ix_r.at[rel, i], x_peer(i, core))

    own_rows = pl.ds(pl.multiple_of(zl * SUB, SUB), SUB)

    def act_copy(j):
        to = y_peer((1 - 2 * core) * ((j + 1) // 2))
        rows = pl.ds(0, ROWS) if j < FULL else own_rows
        return remote(ast.at[to[0], half(j), :, rows], act.at[j, :, rows], act_s.at[j], act_r.at[j], to)

    def z_copy(j, i):
        to = lax.rem(zl + i, 4)
        return remote(sbuf.at[j, to], zrecv.at[j, zl], z_s.at[j, i], z_r.at[j, i], z_peer(i))

    def g_copy(j, i):
        part = whole.at[j, zl] if j < FULL else grads.at[j, :, core, zl]
        return remote(part, part, g_s.at[j, i], g_r.at[j, i], z_peer(i))

    def gc_copy(j):
        part = grads.at[j, :, core]
        return remote(part, part, gc_s.at[j], gc_r.at[j], partner)

    def x_copy(j, i, k):
        to, to_core = lax.rem(x + i, 4), core + k * (1 - 2 * core)
        return remote(
            pbuf.at[j, to_core, to], xrecv.at[j, x, core], x_s.at[j, i, k], x_r.at[j, i, k], x_peer(i, to_core)
        )

    def f_copy(j, side):
        step = ((j + 1) // 2) * (2 * side - 1)
        rows = mine if j == LAST else pl.ds(0, 128)
        return remote(
            fbuf.at[j, side, rows], yrecv.at[j, side, rows], f_s.at[j, side], f_r.at[j, side], y_peer(step)
        )

    def d_copy(side):
        return remote(fbuf.at[LAST, side, other], ydiag.at[side], d_s.at[side], d_r.at[side], diagonal)

    def h_copy(i):
        part = hid.at[pl.ds(FULL, N - FULL), core, zl]
        return remote(part, part, h_s.at[i], h_r.at[i], z_peer(i))

    def hc_copy():
        part = hid.at[:, core]
        return remote(part, part, hc_s.at[0], hc_r.at[0], partner)

    def e_copy():
        return remote(rbuf, hrecv, e_s.at[0], e_r.at[0], far)

    def stage_terms(j):
        term = sum(
            lax.dot_general(og_all[place(j), k], dw_v[k], NT, preferred_element_type=F32) for k in range(2)
        )
        sbuf[j] = term.astype(BF).reshape(4, SUB, cols)
        for i in range(1, 4):
            z_copy(j, i).start()
        oc_copy(j).start()

    def derive(hidden_grad, gate, up):
        sigma = jax.nn.sigmoid(gate)
        silu = gate * sigma
        gate_grad = hidden_grad * up * sigma * (1.0 + gate * (1.0 - sigma))
        return [v.astype(BF) for v in (gate_grad, hidden_grad * silu, silu * up)]

    def stage_act(j):
        for i in range(1, 4):
            z_copy(j, i).wait_recv()
        zrecv[j, zl] = sbuf[j, zl]
        hidden_grad = zrecv[j, 0].astype(F32)
        for i in range(1, 4):
            hidden_grad += zrecv[j, i].astype(F32)
        if j < FULL:
            whole[j, zl] = hidden_grad.astype(BF)
        else:
            gate, up = act[j, 0, own_rows].astype(F32), act[j, 1, own_rows].astype(F32)
            grads[j, 0, core, zl], grads[j, 1, core, zl], hid[j, core, zl] = derive(hidden_grad, gate, up)
        for i in range(1, 4):
            g_copy(j, i).start()

    def stage_input(j):
        for i in range(1, 4):
            g_copy(j, i).wait_recv()
        if j == 0:
            swaps[3].wait_recv()
            swaps[4].wait_recv()
        if j < FULL:
            gate, up = act[j, 0].astype(F32), act[j, 1].astype(F32)
            block = (4, SUB, cols)
            values = derive(whole[j].reshape(ROWS, cols).astype(F32), gate, up)
            grads[j, 0, core], grads[j, 1, core], hid[j, core] = [v.reshape(block) for v in values]
        gate, up = grads[j, 0, core].reshape(ROWS, cols), grads[j, 1, core].reshape(ROWS, cols)
        for k in range(2):
            part = jnp.dot(gate, gw_v[k], preferred_element_type=F32)
            part += jnp.dot(up, uw_v[k], preferred_element_type=F32)
            for i in range(4):
                pbuf[j, k, i] = part[:, i * 128:(i + 1) * 128].astype(BF)
        for i in range(1, 4):
            for k in range(2):
                x_copy(j, i, k).start()
        x_copy(j, 0, 1).start()
        gc_copy(j).start()

    def stage_columns(j):
        x_copy(j, 0, 1).wait_recv()
        for i in range(1, 4):
            for k in range(2):
                x_copy(j, i, k).wait_recv()
        xrecv[j, x, core] = pbuf[j, core, x]
        total = xrecv[j, 0].astype(F32)
        for i in range(1, 4):
            total += xrecv[j, i].astype(F32)
        for side in range(2):
            if j == 0:
                yrecv[0, side] = total[side].T.astype(BF)
            else:
                fbuf[j, side] = total[side].T.astype(BF)
                f_copy(j, side).start()
                if j == LAST:
                    d_copy(side).start()

    def stage_weights(d):
        for j in sorted({max(2 * d - 1, 0), min(2 * d, LAST)}):
            gc_copy(j).wait_recv()
        for rel in sorted({d, (N - d) % N}):
            if rel:
                for i in range(1, 4):
                    ix_copy(rel, i).wait_recv()
            if rel in (0, 4):
                halves = ((max(2 * d - 1, 0), 0), (max(2 * d - 1, 0), 1))
            elif rel < 4:
                halves = ((2 * d - 1, 0), (2 * d, 0))
            else:
                halves = ((2 * d, 1), (2 * d - 1, 1))
            block = inp_all[rel].reshape(2 * ROWS, -1)
            for kind, out in enumerate((out_gate, out_up)):
                part = jnp.concatenate([grads[j, kind, side].reshape(ROWS, cols) for j, side in halves])
                term = lax.dot_general(part, block, TN, preferred_element_type=F32)
                out[...] = out[...] + term if rel else term

    def stage_owner():
        for j in range(1, LAST):
            for side in range(2):
                f_copy(j, side).wait_recv()
        for half in range(2):
            total = yrecv[0, half].astype(F32)
            for j in range(1, LAST):
                total += yrecv[j, (j - 1 + half) % 2].astype(F32)
            total_in[:, half * ROWS:(half + 1) * ROWS] = total
        rbuf[...] = total_in[other].astype(BF)
        e_copy().start()

    def stage_result():
        e_copy().wait_recv()
        for half in range(2):
            f_copy(LAST, half).wait_recv()
            d_copy(half).wait_recv()
        for half in range(2):
            cut = slice(half * ROWS, (half + 1) * ROWS)
            total = total_in[mine, cut] + hrecv[:, cut].astype(F32)
            total += yrecv[LAST, half, mine].astype(F32) + ydiag[half].astype(F32)
            out_in[:, cut] = total.astype(BF)

    def stage_down():
        hc_copy().wait_recv()
        for j in range(N):
            oc_copy(j).wait_recv()
        near = jnp.concatenate([og_all[place(j), core] for j in range(N)])
        far_block = og_far[...].reshape(N * ROWS, -1)
        total = lax.dot_general(
            hid[:, core].reshape(N * ROWS, cols), near, TN, preferred_element_type=F32
        ) + lax.dot_general(
            hid[:, 1 - core].reshape(N * ROWS, cols), far_block, TN, preferred_element_type=F32
        )
        out_down[...] = total

    loads[0].wait()
    loads[1].wait()
    swaps[0].start()
    og_ring(1, core).start()
    swaps[1].start()
    og_ring(2, core).start()
    for load, swap in zip(loads[2:5], swaps[2:]):
        load.wait()
        swap.start()
    swaps[0].wait_recv()
    og_ring(1, 1 - core).start()
    swaps[1].wait_recv()
    og_ring(2, 1 - core).start()
    swaps[2].wait_recv()
    stage_terms(0)
    for i in range(5, 9):
        loads[i].wait()
    for h in range(2):
        for kind in range(2):
            block = araw[kind, h]
            for i in range(N):
                ast[i, h, kind] = block[:, i * cols:(i + 1) * cols]
    act[0] = ast[a, core]
    for j in ACTS_AT[0]:
        act_copy(j).start()
    for copy in loads[9:]:
        copy.wait()

    steps = []

    def og_step(j):
        for k in range(2):
            og_ring(j, k).wait_recv()
        for k in range(2):
            if j + 2 < N:
                og_ring(j + 2, k).start()
        for i in ACTS_AT.get(j, ()):
            act_copy(i).start()
        stage_terms(j)

    def in_step(d):
        if d:
            for side in range(2):
                in_ring(d, side).wait_recv()
        if d < 4:
            for side in range(2):
                in_ring(d + 1, side).start()
        for rel in sorted({d, (N - d) % N} - {0}):
            for i in range(1, 4):
                ix_copy(rel, i).start()

    def act_step(j):
        if j:
            act_copy(j).wait_recv()
        stage_act(j)

    def hid_start():
        for i in range(1, 4):
            h_copy(i).start()

    def hid_share():
        for i in range(1, 4):
            h_copy(i).wait_recv()
        hc_copy().start()

    stages = (og_step, act_step, stage_input, stage_columns, in_step, stage_weights)
    for stage, times in zip(stages, TIMES, strict=True):
        steps += [(when, stage, (j,)) for j, when in enumerate(times) if when is not None]
    once = (hid_start, hid_share, stage_down, stage_owner, stage_result)
    steps += [(when, step, ()) for step, when in zip(once, ONCE, strict=True)]
    for _, step, args in sorted(steps, key=lambda s: s[0]):
        step(*args)

    for j in range(N):
        oc_copy(j).wait_send()
        gc_copy(j).wait_send()
        x_copy(j, 0, 1).wait_send()
        for i in range(1, 4):
            z_copy(j, i).wait_send()
            g_copy(j, i).wait_send()
            for k in range(2):
                x_copy(j, i, k).wait_send()
        if j >= 1:
            act_copy(j).wait_send()
            for side in range(2):
                og_ring(j, side).wait_send()
                f_copy(j, side).wait_send()
    for i in range(1, 4):
        h_copy(i).wait_send()
    for swap in swaps:
        swap.wait_send()
    hc_copy().wait_send()
    e_copy().wait_send()
    for side in range(2):
        d_copy(side).wait_send()
        for d in range(1, 5):
            in_ring(d, side).wait_send()
    for rel in range(1, N):
        for i in range(1, 4):
            ix_copy(rel, i).wait_send()


def deliver(*refs):
    arrays, results, held, sems = refs[0:4], refs[4:8], refs[8:12], refs[12]
    fetch = [pltpu.make_async_copy(arrays[i], held[i], sems.at[0, i]) for i in range(4)]
    store = [pltpu.make_async_copy(held[i], results[i], sems.at[1, i]) for i in range(4)]
    for copy in fetch:
        copy.start()
    for i in range(4):
        fetch[i].wait()
        store[i].start()
    for copy in store:
        copy.wait()


def shards(inputs, out_grad, gate_act, up_act, gate_weight, up_weight, down_weight):
    width, cols = gate_weight.shape
    hidden_cols = gate_act.shape[1]
    dma = pltpu.SemaphoreType.DMA
    scratch = [
        pltpu.VMEM((N + 1, 2, ROWS, width), BF),
        pltpu.VMEM((N, ROWS, width), BF),
        pltpu.VMEM((N, 4, ROWS // 2, width), BF),
        pltpu.VMEM((2, cols, width), BF),
        pltpu.VMEM((2, cols, width), BF),
        pltpu.VMEM((2, cols, width), BF),
        pltpu.VMEM((2, 2, ROWS, hidden_cols), BF),
        pltpu.VMEM((N, 2, 2, ROWS, cols), BF),
        pltpu.VMEM((N, 2, ROWS, cols), BF),
        pltpu.VMEM((N, 4, SUB, cols), BF),
        pltpu.VMEM((N, 4, SUB, cols), BF),
        pltpu.VMEM((N, 4, SUB, cols), BF),
        pltpu.VMEM((N, 2, 2, 4, SUB, cols), BF),
        pltpu.VMEM((N, 2, 4, SUB, cols), BF),
        pltpu.VMEM((N, 2, 4, ROWS, 128), BF),
        pltpu.VMEM((N, 4, 2, ROWS, 128), BF),
        pltpu.VMEM((N, 2, ROWS, 128), BF),
        pltpu.VMEM((N, 2, ROWS, 128), BF),
        pltpu.VMEM((2, 64, ROWS), BF),
        pltpu.VMEM((128, 2 * ROWS), F32),
        pltpu.VMEM((64, 2 * ROWS), BF),
        pltpu.VMEM((64, 2 * ROWS), BF),
        dma((13,)), dma((5,)), dma((5,)),
        dma((N, 2)), dma((N, 2)), dma((N,)), dma((N,)), dma((5, 2)), dma((5, 2)), dma((N, 4)), dma((N, 4)),
        dma((N,)), dma((N,)),
        dma((N, 4)), dma((N, 4)), dma((N, 4)), dma((N, 4)),
        dma((N,)), dma((N,)),
        dma((N, 4, 2)), dma((N, 4, 2)),
        dma((N, 2)), dma((N, 2)),
        dma((4,)), dma((4,)), dma((1,)), dma((1,)), dma((1,)), dma((1,)), dma((2,)), dma((2,)),
    ]
    results = pl.pallas_call(
        kernel,
        out_shape=(
            jax.ShapeDtypeStruct((64, 2 * ROWS), BF),
            jax.ShapeDtypeStruct((cols, width), F32),
            jax.ShapeDtypeStruct((cols, width), F32),
            jax.ShapeDtypeStruct((cols, width), F32),
        ),
        in_specs=[pl.BlockSpec(memory_space=pl.ANY)] * 7,
        out_specs=(pl.BlockSpec(memory_space=pltpu.VMEM),) * 4,
        scratch_shapes=scratch,
        compiler_params=pltpu.CompilerParams(
            collective_id=0, has_side_effects=True, vmem_limit_bytes=56 * 1024 * 1024
        ),
        name="swiglu_backward",
    )(out_grad, inputs, gate_act, up_act, gate_weight.T, up_weight.T, down_weight)
    input_grad, gate_grad, up_grad, down_grad = pl.pallas_call(
        deliver,
        out_shape=tuple(jax.ShapeDtypeStruct(r.shape, r.dtype) for r in results),
        in_specs=[pl.BlockSpec(memory_space=pl.ANY)] * 4,
        out_specs=(pl.BlockSpec(memory_space=pl.ANY),) * 4,
        scratch_shapes=[pltpu.VMEM(r.shape, r.dtype) for r in results] + [dma((2, 4))],
        name="deliver",
    )(*results)
    return (input_grad.T, gate_grad.T, up_grad.T, down_grad)


def solution(mesh):
    in_specs = (
        P("gx", "gy"),
        P("gx", "gy"),
        P("gx", "gz"),
        P("gx", "gz"),
        P("gy", ("gz", "gx")),
        P("gy", ("gz", "gx")),
        P(("gz", "gx"), "gy"),
    )
    out_specs = (
        P("gx", ("gy", "gz")),
        P("gy", ("gz", "gx")),
        P("gy", ("gz", "gx")),
        P(("gz", "gx"), "gy"),
    )
    return jax.shard_map(shards, mesh=mesh, in_specs=in_specs, out_specs=out_specs, check_vma=False)
```
